32 devices in a mesh: groups: 2 (over x), slab: 16 (over z, y, core).
Axes of the slice: x: 2, y: 2, z: 4, core: 2. Of those that a mesh axis runs over, the one named last changes fastest.
Arguments:
- volume_features: bfloat16 [256, 32, 16, 384], P(('groups', 'slab')), parts along dimension 0, may hold values from -6 to 6
- focus_norm_factor: float32 [384], replicated, may hold values from 0.1 to 1.9
- perceptron_norm_factor: float32 [384], replicated, may hold values from 0.1 to 1.9
- courier_triple_projection: bfloat16 [384, 1152], replicated, may hold values from -24 to 24, as said below
- courier_result_projection: bfloat16 [384, 384], replicated, may hold values from -0.3125 to 0.3125
- region_triple_projection: bfloat16 [384, 1152], replicated, may hold values from -24 to 24, as said below
- region_result_projection: bfloat16 [384, 384], replicated, may hold values from -0.3125 to 0.3125
- perceptron_entry_projection: bfloat16 [384, 1536], replicated, may hold values from -0.3125 to 0.3125
- perceptron_exit_projection: bfloat16 [1536, 384], replicated, may hold values from -0.15625 to 0.15625
Outputs:
- result: bfloat16 [256, 32, 16, 384], P(('groups', 'slab')), parts along dimension 0
The draws below stay inside these ranges and needn't reach their ends.
There are 2 independent parts, one for each index of `groups`. The reference program is written for one: setup_inputs(seed, part) draws one part's arguments, and reference() takes and returns one part's arrays. A program takes and returns all parts, laid end to end along the dimension named above; an argument that names none is the same for every part. Nothing has to cross between parts.
Inputs may be any that keep to these rules, and one draw needn't show every extreme that they name: `courier_triple_projection`: a projection for inputs of 384 features. `region_triple_projection`: a projection for inputs of 384 features.
All inputs are finite; a program needn't handle non-finite values.
Results may differ from the reference program's by a relative error of at most 0.0063.
Values may be sent and summed in bfloat16 or wider, within the bound.
A program may use at most 128 MiB of HBM per device.

```python
import jax
import jax.numpy as jnp
from jax import lax

EMBED_BREADTH = 384
FOCUS_BRANCHES = 12
BRANCH_BREADTH = 32
FF = 1536
WIN = 8
NY = 32
NX = 16
NZ = 128


def drawn_projection(key):
    base_key = jax.random.fold_in(key, 0)
    base = jnp.clip(jax.random.normal(base_key, (EMBED_BREADTH, 3 * EMBED_BREADTH), jnp.float32), -6.0, 6.0) * EMBED_BREADTH ** (-0.5)
    return base.astype(jnp.bfloat16)


def draw_courier_triple_projection(key, part):
    return drawn_projection(jax.random.fold_in(key, 23))


def draw_region_triple_projection(key, part):
    return drawn_projection(jax.random.fold_in(key, 11))


def level_of(rng, extent, cuts, least, high):
    def one(axis_at, blocks):
        heights = jax.random.uniform(jax.random.fold_in(jax.random.fold_in(rng, 6), axis_at), (blocks,), jnp.float32, least / len(cuts), high / len(cuts))
        return jnp.repeat(jnp.exp(heights), extent[axis_at] // blocks).reshape((-1,) + (1,) * (len(extent) - axis_at - 1))

    loudness = one(*cuts[0])
    for cut in cuts[1:]:
        loudness = loudness * one(*cut)
    return loudness


def bell_draw(key, dims, width, limit, cuts=(), kind=jnp.bfloat16):
    values = width * jax.random.normal(key, dims, jnp.float32)
    if cuts:
        values = values * level_of(key, dims, cuts, -0.22, 0.18)
    return jnp.clip(values, -limit, limit).astype(kind)


def setup_inputs(seed: int = 0, part: int = 0) -> dict:
    keys = jax.random.split(jax.random.key(seed), 10)
    part_keys = jax.random.split(jax.random.fold_in(keys[9], part), 10)
    return {
        "volume_features": bell_draw(part_keys[0], (NZ, NY, NX, EMBED_BREADTH), 1.0, 6.0, ((0, 16),)),
        "focus_norm_factor": jnp.clip(1.0 + 0.18 * jax.random.normal(keys[1], (EMBED_BREADTH,), jnp.float32), 0.1, 1.9),
        "perceptron_norm_factor": jnp.clip(1.0 + 0.18 * jax.random.normal(keys[2], (EMBED_BREADTH,), jnp.float32), 0.1, 1.9),
        "courier_triple_projection": draw_courier_triple_projection(jax.random.fold_in(keys[9], 71), part),
        "courier_result_projection": bell_draw(keys[4], (EMBED_BREADTH, EMBED_BREADTH), EMBED_BREADTH ** -0.5, 0.3125),
        "region_triple_projection": draw_region_triple_projection(jax.random.fold_in(keys[9], 71), part),
        "region_result_projection": bell_draw(keys[6], (EMBED_BREADTH, EMBED_BREADTH), EMBED_BREADTH ** -0.5, 0.3125),
        "perceptron_entry_projection": bell_draw(keys[7], (EMBED_BREADTH, FF), EMBED_BREADTH ** -0.5, 0.3125),
        "perceptron_exit_projection": bell_draw(keys[8], (FF, EMBED_BREADTH), FF ** -0.5, 0.15625),
    }


def normalized_entries(values, gain):
    values = values.astype(jnp.float32)
    centre = lax.optimization_barrier(jnp.mean(values, axis=-1, keepdims=True))
    shifted = values - centre
    spread = lax.optimization_barrier(jnp.mean(shifted * shifted, axis=-1, keepdims=True))
    return shifted * lax.rsqrt(spread + 1e-05) * gain.astype(jnp.float32)

def to_windows(scanned_solid, cubic_patch):
    planes, height, across, channels = scanned_solid.shape
    blocks = scanned_solid.reshape(planes // cubic_patch, cubic_patch, height // cubic_patch, cubic_patch, across // cubic_patch, cubic_patch, channels)
    return blocks.transpose(0, 2, 4, 1, 3, 5, 6).reshape(-1, cubic_patch ** 3, channels)

def from_windows(windows, planes, height, across, cubic_patch):
    channels = windows.shape[-1]
    blocks = windows.reshape(planes // cubic_patch, height // cubic_patch, across // cubic_patch, cubic_patch, cubic_patch, cubic_patch, channels)
    return blocks.transpose(0, 3, 1, 4, 2, 5, 6).reshape(planes, height, across, channels)

def window_local(stacked_entries, labels):
    count = stacked_entries.shape[0]
    similarity_multiplier = BRANCH_BREADTH ** (-0.5)
    asking_table = stacked_entries[:, :EMBED_BREADTH].reshape(count, FOCUS_BRANCHES, BRANCH_BREADTH).astype(jnp.float32)
    source_table = stacked_entries[:, EMBED_BREADTH:2 * EMBED_BREADTH].reshape(count, FOCUS_BRANCHES, BRANCH_BREADTH).astype(jnp.float32)
    value_rows = stacked_entries[:, 2 * EMBED_BREADTH:].reshape(count, FOCUS_BRANCHES, BRANCH_BREADTH).astype(jnp.float32)
    similarity_table = jnp.einsum('cfm,rfm->fcr', asking_table, source_table, precision=lax.Precision.HIGHEST) * similarity_multiplier
    allowed = labels[:, None] == labels[None, :]
    ongoing_peak = lax.optimization_barrier(jnp.max(jnp.where(allowed[None], similarity_table, -jnp.inf), axis=-1))
    weights = jnp.where(allowed[None], jnp.exp(similarity_table - ongoing_peak[..., None]), 0.0)
    ongoing_totals = lax.optimization_barrier(jnp.sum(weights, axis=-1))
    rounded = weights.astype(jnp.bfloat16).astype(jnp.float32)
    interim_result = jnp.einsum('tlq,qto->lto', rounded, value_rows, precision=lax.Precision.HIGHEST)
    return (interim_result, ongoing_totals, ongoing_peak)

def merge_courier(interim_result, ongoing_totals, ongoing_peak, stacked_entries, courier_lookup_entries, courier_content_entries):
    count = stacked_entries.shape[0]
    similarity_multiplier = BRANCH_BREADTH ** (-0.5)
    asking_table = stacked_entries[:, :EMBED_BREADTH].reshape(count, FOCUS_BRANCHES, BRANCH_BREADTH).astype(jnp.float32)
    courier_affinity = lax.optimization_barrier(jnp.sum(asking_table * courier_lookup_entries.astype(jnp.float32)[None], axis=-1)) * similarity_multiplier
    tile_peak = ongoing_peak.T
    tile_total = ongoing_totals.T
    ceiling_limit = jnp.maximum(tile_peak, courier_affinity)
    tile_correction = jnp.exp(tile_peak - ceiling_limit)
    courier_correction_factor = jnp.exp(courier_affinity - ceiling_limit)
    dividend_accumulator = interim_result * tile_correction[..., None] + courier_correction_factor[..., None] * courier_content_entries.astype(jnp.float32)[None]
    divisor_total = tile_total * tile_correction + courier_correction_factor
    return (dividend_accumulator / divisor_total[..., None]).reshape(count, EMBED_BREADTH).astype(jnp.bfloat16)

def reference(volume_features, focus_norm_factor, perceptron_norm_factor, courier_triple_projection, courier_result_projection, region_triple_projection, region_result_projection, perceptron_entry_projection, perceptron_exit_projection):
    half_window = WIN // 2
    similarity_multiplier = BRANCH_BREADTH ** (-0.5)
    rolled = jnp.roll(volume_features, (-half_window, -half_window, -half_window), axis=(0, 1, 2))
    z_label = (jnp.arange(NZ) >= NZ - half_window).astype(jnp.int32)
    y_label = (jnp.arange(NY) >= NY - half_window).astype(jnp.int32)
    x_label = (jnp.arange(NX) >= NX - half_window).astype(jnp.int32)
    labels = z_label[:, None, None] * 4 + y_label[None, :, None] * 2 + x_label[None, None, :]
    region_features = to_windows(rolled, WIN)
    region_identifiers = to_windows(labels[..., None], WIN)[..., 0]
    region_number = region_features.shape[0]
    courier_features = lax.optimization_barrier(jnp.mean(region_features.astype(jnp.float32), axis=1))
    courier_normalized_entries = normalized_entries(courier_features, focus_norm_factor).astype(jnp.bfloat16)
    courier_mapped = jnp.dot(courier_normalized_entries, courier_triple_projection, preferred_element_type=jnp.float32).astype(jnp.bfloat16)
    relay_asking_elements = courier_mapped[:, :EMBED_BREADTH].reshape(region_number, FOCUS_BRANCHES, BRANCH_BREADTH).astype(jnp.float32)
    relay_source_slice = courier_mapped[:, EMBED_BREADTH:2 * EMBED_BREADTH].reshape(region_number, FOCUS_BRANCHES, BRANCH_BREADTH).astype(jnp.float32)
    courier_content_tile = courier_mapped[:, 2 * EMBED_BREADTH:].reshape(region_number, FOCUS_BRANCHES, BRANCH_BREADTH).astype(jnp.float32)
    similarity_table = jnp.einsum('cfm,rfm->fcr', relay_asking_elements, relay_source_slice, precision=lax.Precision.HIGHEST) * similarity_multiplier
    softmax_weights_grid = jax.nn.softmax(similarity_table, axis=-1)
    courier_merge = jnp.einsum('tlq,qto->lto', softmax_weights_grid, courier_content_tile, precision=lax.Precision.HIGHEST)
    courier_merge = courier_merge.reshape(region_number, EMBED_BREADTH).astype(jnp.bfloat16)
    courier_delta_vector = jnp.dot(courier_merge, courier_result_projection, preferred_element_type=jnp.float32)
    revised_entries = courier_features + courier_delta_vector
    revised_normalized_entries = normalized_entries(revised_entries, focus_norm_factor).astype(jnp.bfloat16)
    courier_lookup_content = jnp.dot(revised_normalized_entries, region_triple_projection[:, EMBED_BREADTH:], preferred_element_type=jnp.float32).astype(jnp.bfloat16)
    courier_lookup_entries = courier_lookup_content[:, :EMBED_BREADTH].reshape(region_number, FOCUS_BRANCHES, BRANCH_BREADTH)
    courier_content_entries = courier_lookup_content[:, EMBED_BREADTH:].reshape(region_number, FOCUS_BRANCHES, BRANCH_BREADTH)
    tok_normed = normalized_entries(region_features, focus_norm_factor).astype(jnp.bfloat16)
    stacked_entries = jnp.dot(tok_normed.reshape(-1, EMBED_BREADTH), region_triple_projection, preferred_element_type=jnp.float32).astype(jnp.bfloat16)
    stacked_entries = stacked_entries.reshape(region_number, WIN ** 3, 3 * EMBED_BREADTH)

    def lone_region(region_members):
        interim_result, ongoing_totals, ongoing_peak = window_local(region_members[0], region_members[1])
        return merge_courier(interim_result, ongoing_totals, ongoing_peak, region_members[0], region_members[2], region_members[3])
    mixed_entries = lax.map(lone_region, (stacked_entries, region_identifiers, courier_lookup_entries, courier_content_entries))
    mapped_entries = jnp.dot(mixed_entries.reshape(-1, EMBED_BREADTH), region_result_projection, preferred_element_type=jnp.float32)
    mapped_entries = mapped_entries.reshape(region_number, WIN ** 3, EMBED_BREADTH)
    merged_entries = (region_features.astype(jnp.float32) + mapped_entries + courier_delta_vector[:, None, :]).astype(jnp.bfloat16)
    flat = merged_entries.reshape(-1, EMBED_BREADTH)
    normed = normalized_entries(flat, perceptron_norm_factor).astype(jnp.bfloat16)
    hidden = jax.nn.gelu(jnp.dot(normed, perceptron_entry_projection, preferred_element_type=jnp.float32), approximate=True).astype(jnp.bfloat16)
    block_out = (flat.astype(jnp.float32) + jnp.dot(hidden, perceptron_exit_projection, preferred_element_type=jnp.float32)).astype(jnp.bfloat16)
    scanned_solid = from_windows(block_out.reshape(region_number, WIN ** 3, EMBED_BREADTH), NZ, NY, NX, WIN)
    return jnp.roll(scanned_solid, (half_window, half_window, half_window), axis=(0, 1, 2))
```

```python
import functools

import jax
import jax.numpy as jnp
from jax import lax
from jax.experimental import pallas as pl
from jax.experimental.pallas import tpu as pltpu
from jax.sharding import PartitionSpec as P

C = 384
HEADS = 12
HD = 32
WIN = 8
HALF = 4
GROUPS = C // 128
BIG = 2.0**100
LOG2E = 1.4426950408889634


def shifted(value, axis, steps):
    count = lax.axis_size(axis)
    pairs = [(source, (source + steps) % count) for source in range(count)]
    return lax.ppermute(value, axis, pairs)


def norm(values, gain):
    values = values.astype(jnp.float32)
    centre = jnp.mean(values, axis=-1, keepdims=True)
    moved = values - centre
    spread = jnp.mean(moved * moved, axis=-1, keepdims=True)
    return moved * lax.rsqrt(spread + 1e-05) * gain


def dot_t(a, b):
    return lax.dot_general(a, b, (((1,), (1,)), ((), ())), preferred_element_type=jnp.float32)


def strip_kernel(
    first,
    strips,
    last_ref,
    loc_a,
    loc_b,
    halo_a,
    halo_b,
    g1,
    g2,
    wqkv,
    wo,
    w1,
    w2,
    delta,
    kc,
    vc,
    out_loc,
    out_halo,
    x_s,
    qkv_s,
    att_s,
    y_s,
):
    strip = pl.program_id(0) + first
    rows = 2 * WIN**3
    half = WIN**3
    tokens = jnp.concatenate(
        [r[...].reshape(rows // 4, C).astype(jnp.float32) for r in (loc_a, loc_b, halo_a, halo_b)],
        axis=0,
    )
    tokens = pltpu.roll(tokens, rows - HALF, 0).reshape(rows // 16, 2, 8, C)
    gain1 = g1[...]
    for w in range(2):
        x_w = tokens[:, w].reshape(half, C)
        x_s[w] = x_w
        n_w = norm(x_w, gain1).astype(jnp.bfloat16)
        for part in range(3):
            proj = jnp.dot(
                n_w, wqkv[:, part * C : (part + 1) * C], preferred_element_type=jnp.float32
            )
            if part == 0:
                proj = proj * (HD**-0.5 * LOG2E)
            proj = proj.astype(jnp.bfloat16)
            for g in range(GROUPS):
                qkv_s[part, w, g] = proj[:, g * 128 : (g + 1) * 128]

    lane = lax.broadcasted_iota(jnp.int32, (1, 128), 1)
    zflag = last_ref[0]
    yflag = jnp.where(strip == strips - 1, 1, 0)

    def attend(step, carry):
        w = step // GROUPS
        g = step % GROUPS
        row = lax.broadcasted_iota(jnp.int32, (half, 128), 0)
        col = lax.broadcasted_iota(jnp.int32, (half, 128), 1)
        t = ((row // 8) * 16 + row % 8 + w * 8 + HALF) & (rows - 1)
        label = (
            (t // half) * 4 * zflag
            + ((t // (half // 2)) & 1) * 2 * yflag
            + jnp.where((t & 15) < HALF, w, 0)
        )
        same = label == col
        feat_q = jnp.where(same, 0.0, -BIG).astype(jnp.bfloat16)
        feat_k = jnp.where(same, 1.0, 0.0).astype(jnp.bfloat16)
        q4 = qkv_s[0, w, g]
        k4 = qkv_s[1, w, g]
        v4 = qkv_s[2, w, g]
        k_aug = jnp.concatenate([k4, feat_k], axis=1)
        acc = jnp.zeros((half, 256), jnp.float32)
        peak = jnp.zeros((half, 128), jnp.float32)
        zero = jnp.zeros((), jnp.bfloat16)
        for h in range(4):
            mine = (lane // HD) == h
            mask = jnp.where(mine, 1.0, 0.0).astype(jnp.bfloat16)
            q_aug = jnp.concatenate([q4 * mask, feat_q], axis=1)
            s = dot_t(q_aug, k_aug)
            m = jnp.max(s, axis=1, keepdims=True)
            p = jnp.exp2(s - m).astype(jnp.bfloat16)
            v_aug = jnp.concatenate([v4 * mask, jnp.broadcast_to(mask, (half, 128))], axis=1)
            acc = acc + jnp.dot(p, v_aug, preferred_element_type=jnp.float32)
            peak = jnp.where(mine, m, peak)
        kcw = kc[0, pl.ds(w, 1), g]
        vcw = vc[0, pl.ds(w, 1), g]
        r128 = lax.broadcasted_iota(jnp.int32, (128, 128), 0)
        c128 = lax.broadcasted_iota(jnp.int32, (128, 128), 1)
        k_mat = jnp.where(r128 // HD == c128 // HD, kcw, 0.0).astype(jnp.bfloat16)
        c4 = dot_t(q4, k_mat)
        top = jnp.maximum(peak, c4)
        a = jnp.exp2(peak - top)
        e = jnp.exp2(c4 - top)
        att = (acc[:, :128] * a + e * vcw) / (acc[:, 128:] * a + e)
        att_s[w, g] = att.astype(jnp.bfloat16)
        return carry

    lax.fori_loop(0, 2 * GROUPS, attend, 0)

    gain2 = g2[...]
    tile = half // 2

    def finish(step, carry):
        w = step // 2
        part = step % 2
        at = pl.ds(pl.multiple_of(part * tile, tile), tile)
        att = jnp.concatenate([att_s[w, g, at] for g in range(GROUPS)], axis=1)
        mixed = x_s[w, at] + jnp.dot(att, wo[...], preferred_element_type=jnp.float32)
        mixed = (mixed + delta[0, pl.ds(w, 1)]).astype(jnp.bfloat16).astype(jnp.float32)
        n = norm(mixed, gain2).astype(jnp.bfloat16)
        u = jnp.dot(n, w1[...], preferred_element_type=jnp.float32)
        hidden = 0.5 * u * (1.0 + jnp.tanh((2.0 / jnp.pi) ** 0.5 * (u + 0.044715 * (u * u * u))))
        out = mixed + jnp.dot(
            hidden.astype(jnp.bfloat16), w2[...], preferred_element_type=jnp.float32
        )
        y_s[pl.ds(part * (tile // 8), tile // 8), w] = out.reshape(tile // 8, 8, C)
        return carry

    lax.fori_loop(0, 4, finish, 0)
    done = pltpu.roll(y_s[...].reshape(rows, C), HALF, 0).astype(jnp.bfloat16)
    done = done.reshape(4, HALF, HALF * 16, C)
    ya = 2 * pl.program_id(0)
    out_loc[:, ya] = done[0]
    out_loc[:, ya + 1] = done[1]
    out_halo[:, ya] = done[2]
    out_halo[:, ya + 1] = done[3]


def strips_call(first, count, strips, last, volume, halo, halo_first, g1, g2, ws, delta, kc, vc):
    yh = 2 * strips

    def block(plane, offset):
        return pl.BlockSpec(
            (HALF, 1, HALF * 16, C), lambda b: (plane, (2 * (b + first) + offset) % yh, 0, 0)
        )

    def halo_block(offset):
        return pl.BlockSpec((HALF, 1, HALF * 16, C), lambda b: (0, 2 * b + offset + halo_first, 0, 0))

    def whole(a):
        return pl.BlockSpec(a.shape, lambda b: (0,) * a.ndim)

    per = [
        pl.BlockSpec((1,) + a.shape[1:], lambda b, n=a.ndim: (b + first,) + (0,) * (n - 1))
        for a in (delta, kc, vc)
    ]
    half = WIN**3
    shape = jax.ShapeDtypeStruct((HALF, 2 * count, HALF * 16, C), jnp.bfloat16)
    out_spec = pl.BlockSpec(shape.shape, lambda b: (0, 0, 0, 0))
    flops = count * 2 * half * 2 * (C * 3 * C + C * C + 2 * C * 4 * C + HEADS * half * 320)
    return pl.pallas_call(
        functools.partial(strip_kernel, first, strips),
        grid=(count,),
        out_shape=(shape, shape),
        in_specs=[
            pl.BlockSpec(memory_space=pltpu.SMEM),
            block(1, 1),
            block(1, 2),
            halo_block(0),
            halo_block(1),
            whole(g1),
            whole(g2),
        ]
        + [whole(w) for w in ws]
        + per,
        out_specs=(out_spec, out_spec),
        scratch_shapes=[
            pltpu.VMEM((2, half, C), jnp.float32),
            pltpu.VMEM((3, 2, GROUPS, half, 128), jnp.bfloat16),
            pltpu.VMEM((2, GROUPS, half, 128), jnp.bfloat16),
            pltpu.VMEM((2 * half // 16, 2, 8, C), jnp.float32),
        ],
        compiler_params=pltpu.CompilerParams(
            dimension_semantics=("arbitrary",), vmem_limit_bytes=48 * 1024 * 1024
        ),
        cost_estimate=pl.CostEstimate(
            flops=flops,
            bytes_accessed=count * 4 * 2 * half * C * 2,
            transcendentals=count * 2 * half * (HEADS * half + 4 * C),
        ),
        name="strips",
    )(last, volume, volume, halo, halo, g1, g2, *ws, delta, kc, vc)


def carriers(volume, g1, wc, wco, wr):
    planes, yh = volume.shape[:2]
    strips = yh // 2
    parts = volume.astype(jnp.float32).reshape(2, HALF, yh, HALF, 16, C).sum(axis=(1, 3))
    inner = parts[:, :, 4:12].sum(axis=2)
    outer = parts[:, :, :4].sum(axis=2) + parts[:, :, 12:].sum(axis=2)
    sums = jnp.stack([inner, outer], axis=2)
    sums = jnp.roll(sums, -1, axis=1).reshape(2, strips, 2, 2, C).sum(axis=2)
    sums = sums.reshape(2, strips * 2, C)
    arrived = shifted(sums[0], "slab", -1)
    carrier = (sums[1] + arrived) * (1.0 / WIN**3)
    count = carrier.shape[0]
    normed = norm(carrier, g1).astype(jnp.bfloat16)
    proj = jnp.dot(normed, wc, preferred_element_type=jnp.float32).astype(jnp.bfloat16)
    asking = proj[:, :C].reshape(count, HEADS, HD)
    everyone = lax.all_gather(proj[:, C:], "slab", axis=0, tiled=True)
    keys = everyone[:, :C].reshape(-1, HEADS, HD)
    values = everyone[:, C:].reshape(-1, HEADS, HD).astype(jnp.float32)
    s = jnp.einsum("chd,rhd->hcr", asking, keys, preferred_element_type=jnp.float32) * HD**-0.5
    weights = jax.nn.softmax(s, axis=-1)
    mix = jnp.einsum("hcr,rhd->chd", weights, values, precision=lax.Precision.HIGHEST)
    mix = mix.reshape(count, C).astype(jnp.bfloat16)
    delta = jnp.dot(mix, wco, preferred_element_type=jnp.float32)
    kv = jnp.dot(
        norm(carrier + delta, g1).astype(jnp.bfloat16), wr[:, C:], preferred_element_type=jnp.float32
    ).astype(jnp.bfloat16)
    kv = kv.astype(jnp.float32)
    kc = kv[:, :C].reshape(strips, 2, GROUPS, 128)
    vc = kv[:, C:].reshape(strips, 2, GROUPS, 128)
    return delta.reshape(strips, 2, C), kc, vc


CALLS = 1


def body(volume_features, g1, g2, wc, wco, wr, wro, w1, w2):
    planes, ny, nx, channels = volume_features.shape
    yh = ny // HALF
    strips = yh // 2
    volume = volume_features.reshape(planes, yh, HALF * nx, channels)
    position = lax.axis_index("slab")
    last = (position == lax.axis_size("slab") - 1).astype(jnp.int32).reshape(1)
    sent = jnp.concatenate([volume[:HALF, 1:], volume[:HALF, :1]], axis=1)
    per = strips // CALLS
    halos = [shifted(sent[:, 2 * per * i : 2 * per * (i + 1)], "slab", -1) for i in range(CALLS)]
    delta, kc, vc = carriers(volume, g1, wc, wco, wr)
    gains = (g1.reshape(1, channels), g2.reshape(1, channels))
    ws = (wr, wro, w1, w2)
    local, returned = [], []
    for i in range(CALLS):
        out_loc, out_halo = strips_call(
            i * per, per, strips, last, volume, halos[i], 0, *gains, ws, delta, kc, vc
        )
        local.append(out_loc)
        returned.append(shifted(out_halo, "slab", 1))
    local = jnp.concatenate(local, axis=1)
    returned = jnp.concatenate(returned, axis=1)
    done = jnp.concatenate([returned, local], axis=0)
    done = jnp.concatenate([done[:, -1:], done[:, :-1]], axis=1)
    return done.reshape(volume_features.shape)


def solution(mesh):
    placed = (P(("groups", "slab"), None, None, None),) + (P(),) * 8
    return jax.shard_map(
        body,
        mesh=mesh,
        in_specs=placed,
        out_specs=P(("groups", "slab"), None, None, None),
        check_vma=False,
    )
```

```python
import functools

import jax
import jax.numpy as jnp
from jax import lax
from jax.experimental import pallas as pl
from jax.experimental.pallas import tpu as pltpu
from jax.sharding import PartitionSpec as P

C = 384
HEADS = 12
HD = 32
WIN = 8
HALF = 4
GROUPS = C // 128
BIG = 2.0**100
LOG2E = 1.4426950408889634


def shifted(value, axis, steps):
    count = lax.axis_size(axis)
    pairs = [(source, (source + steps) % count) for source in range(count)]
    return lax.ppermute(value, axis, pairs)


def norm(values, gain):
    values = values.astype(jnp.float32)
    centre = jnp.mean(values, axis=-1, keepdims=True)
    moved = values - centre
    spread = jnp.mean(moved * moved, axis=-1, keepdims=True)
    return moved * lax.rsqrt(spread + 1e-05) * gain


def dot_t(a, b):
    return lax.dot_general(a, b, (((1,), (1,)), ((), ())), preferred_element_type=jnp.float32)


def row_of(values, row):
    at = lax.broadcasted_iota(jnp.int32, values.shape, 0)
    return jnp.sum(jnp.where(at == row, values, 0.0), axis=0, keepdims=True)


def strip_kernel(
    first,
    strips,
    last_ref,
    loc_a,
    loc_b,
    halo_a,
    halo_b,
    g1,
    g2,
    wqkv,
    wo,
    w1,
    w2,
    delta,
    kc,
    vc,
    out_loc,
    out_halo,
    x_s,
    qkv_s,
    att_s,
    y_s,
):
    strip = pl.program_id(0) + first
    rows = 2 * WIN**3
    half = WIN**3
    tokens = jnp.concatenate(
        [r[...].reshape(rows // 4, C).astype(jnp.float32) for r in (loc_a, loc_b, halo_a, halo_b)],
        axis=0,
    )
    tokens = pltpu.roll(tokens, rows - HALF, 0).reshape(rows // 16, 2, 8, C)
    gain1 = g1[...]
    for w in range(2):
        x_w = tokens[:, w].reshape(half, C)
        x_s[w] = x_w
        n_w = norm(x_w, gain1).astype(jnp.bfloat16)
        for part in range(3):
            proj = jnp.dot(
                n_w, wqkv[:, part * C : (part + 1) * C], preferred_element_type=jnp.float32
            )
            if part == 0:
                proj = proj * (HD**-0.5 * LOG2E)
            proj = proj.astype(jnp.bfloat16)
            for g in range(GROUPS):
                qkv_s[part, w, g] = proj[:, g * 128 : (g + 1) * 128]

    lane = lax.broadcasted_iota(jnp.int32, (1, 128), 1)
    zflag = last_ref[0]
    yflag = jnp.where(strip == strips - 1, 1, 0)

    def attend(step, carry):
        w = step // GROUPS
        g = step % GROUPS
        row = lax.broadcasted_iota(jnp.int32, (half, 128), 0)
        col = lax.broadcasted_iota(jnp.int32, (half, 128), 1)
        t = ((row // 8) * 16 + row % 8 + w * 8 + HALF) & (rows - 1)
        label = (
            (t // half) * 4 * zflag
            + ((t // (half // 2)) & 1) * 2 * yflag
            + jnp.where((t & 15) < HALF, w, 0)
        )
        same = label == col
        feat_q = jnp.where(same, 0.0, -BIG).astype(jnp.bfloat16)
        feat_k = jnp.where(same, 1.0, 0.0).astype(jnp.bfloat16)
        q4 = qkv_s[0, w, g]
        k4 = qkv_s[1, w, g]
        v4 = qkv_s[2, w, g]
        k_aug = jnp.concatenate([k4, feat_k], axis=1)
        acc = jnp.zeros((half, 256), jnp.float32)
        peak = jnp.zeros((half, 128), jnp.float32)
        zero = jnp.zeros((), jnp.bfloat16)
        for h in range(4):
            mine = (lane // HD) == h
            mask = jnp.where(mine, 1.0, 0.0).astype(jnp.bfloat16)
            q_aug = jnp.concatenate([q4 * mask, feat_q], axis=1)
            s = dot_t(q_aug, k_aug)
            m = jnp.max(s, axis=1, keepdims=True)
            p = jnp.exp2(s - m).astype(jnp.bfloat16)
            v_aug = jnp.concatenate([v4 * mask, jnp.broadcast_to(mask, (half, 128))], axis=1)
            acc = acc + jnp.dot(p, v_aug, preferred_element_type=jnp.float32)
            peak = jnp.where(mine, m, peak)
        lanes = pl.ds(pl.multiple_of(g * 128, 128), 128)
        kcw = row_of(kc[:, lanes], 2 * strip + w)
        vcw = row_of(vc[:, lanes], 2 * strip + w)
        r128 = lax.broadcasted_iota(jnp.int32, (128, 128), 0)
        c128 = lax.broadcasted_iota(jnp.int32, (128, 128), 1)
        k_mat = jnp.where(r128 // HD == c128 // HD, kcw, 0.0).astype(jnp.bfloat16)
        c4 = dot_t(q4, k_mat)
        top = jnp.maximum(peak, c4)
        a = jnp.exp2(peak - top)
        e = jnp.exp2(c4 - top)
        att = (acc[:, :128] * a + e * vcw) / (acc[:, 128:] * a + e)
        att_s[w, g] = att.astype(jnp.bfloat16)
        return carry

    lax.fori_loop(0, 2 * GROUPS, attend, 0)

    gain2 = g2[...]
    tile = half // 2

    def finish(step, carry):
        w = step // 2
        part = step % 2
        at = pl.ds(pl.multiple_of(part * tile, tile), tile)
        att = jnp.concatenate([att_s[w, g, at] for g in range(GROUPS)], axis=1)
        mixed = x_s[w, at] + jnp.dot(att, wo[...], preferred_element_type=jnp.float32)
        mixed = (mixed + row_of(delta[...], 2 * strip + w)).astype(jnp.bfloat16).astype(jnp.float32)
        n = norm(mixed, gain2).astype(jnp.bfloat16)
        u = jnp.dot(n, w1[...], preferred_element_type=jnp.float32)
        hidden = 0.5 * u * (1.0 + jnp.tanh((2.0 / jnp.pi) ** 0.5 * (u + 0.044715 * (u * u * u))))
        out = mixed + jnp.dot(
            hidden.astype(jnp.bfloat16), w2[...], preferred_element_type=jnp.float32
        )
        y_s[pl.ds(part * (tile // 8), tile // 8), w] = out.reshape(tile // 8, 8, C)
        return carry

    lax.fori_loop(0, 4, finish, 0)
    done = pltpu.roll(y_s[...].reshape(rows, C), HALF, 0).astype(jnp.bfloat16)
    done = done.reshape(4, HALF, HALF * 16, C)
    ya = 2 * pl.program_id(0)
    out_loc[:, ya] = done[0]
    out_loc[:, ya + 1] = done[1]
    out_halo[:, ya] = done[2]
    out_halo[:, ya + 1] = done[3]


def strips_call(first, count, strips, last, volume, halo, halo_first, g1, g2, ws, delta, kc, vc):
    yh = 2 * strips

    def block(plane, offset):
        return pl.BlockSpec(
            (HALF, 1, HALF * 16, C), lambda b: (plane, (2 * (b + first) + offset) % yh, 0, 0)
        )

    def halo_block(offset):
        return pl.BlockSpec((HALF, 1, HALF * 16, C), lambda b: (0, 2 * b + offset + halo_first, 0, 0))

    def whole(a):
        return pl.BlockSpec(a.shape, lambda b: (0,) * a.ndim)

    half = WIN**3
    shape = jax.ShapeDtypeStruct((HALF, 2 * count, HALF * 16, C), jnp.bfloat16)
    out_spec = pl.BlockSpec(shape.shape, lambda b: (0, 0, 0, 0))
    flops = count * 2 * half * 2 * (C * 3 * C + C * C + 2 * C * 4 * C + HEADS * half * 320)
    return pl.pallas_call(
        functools.partial(strip_kernel, first, strips),
        grid=(count,),
        out_shape=(shape, shape),
        in_specs=[
            pl.BlockSpec(memory_space=pltpu.SMEM),
            block(1, 1),
            block(1, 2),
            halo_block(0),
            halo_block(1),
            whole(g1),
            whole(g2),
        ]
        + [whole(w) for w in (*ws, delta, kc, vc)],
        out_specs=(out_spec, out_spec),
        scratch_shapes=[
            pltpu.VMEM((2, half, C), jnp.float32),
            pltpu.VMEM((3, 2, GROUPS, half, 128), jnp.bfloat16),
            pltpu.VMEM((2, GROUPS, half, 128), jnp.bfloat16),
            pltpu.VMEM((2 * half // 16, 2, 8, C), jnp.float32),
        ],
        compiler_params=pltpu.CompilerParams(
            dimension_semantics=("arbitrary",), vmem_limit_bytes=48 * 1024 * 1024
        ),
        cost_estimate=pl.CostEstimate(
            flops=flops,
            bytes_accessed=count * 4 * 2 * half * C * 2,
            transcendentals=count * 2 * half * (HEADS * half + 4 * C),
        ),
        name="strips",
    )(last, volume, volume, halo, halo, g1, g2, *ws, delta, kc, vc)


def sums_kernel(volume, out):
    planes = volume.shape[0]
    block = volume[:, 0].astype(jnp.float32)
    out[0] = block.reshape(planes // HALF, HALF * HALF, 16, C).sum(axis=1)


def half_sums(volume):
    planes, yh = volume.shape[:2]
    return pl.pallas_call(
        sums_kernel,
        grid=(yh,),
        out_shape=jax.ShapeDtypeStruct((yh, planes // HALF, 16, C), jnp.float32),
        in_specs=[pl.BlockSpec((planes, 1, HALF * 16, C), lambda y: (0, y, 0, 0))],
        out_specs=pl.BlockSpec((1, planes // HALF, 16, C), lambda y: (y, 0, 0, 0)),
        cost_estimate=pl.CostEstimate(
            flops=2 * volume.size, bytes_accessed=2 * volume.size, transcendentals=0
        ),
        name="half_sums",
    )(volume)


def carrier_kernel(
    n, parts, g1, wc, wco, wr, delta_out, kc_out, vc_out,
    sums, arrived, everyone, halo_send, halo_recv, send_sem, recv_sem,
):
    me = lax.axis_index("slab")
    barrier = pltpu.get_barrier_semaphore()

    @pl.loop(1, n)
    def _(d):
        pl.semaphore_signal(
            barrier, inc=1, device_id={"slab": lax.rem(me + d, n)}, device_id_type=pl.DeviceIdType.MESH
        )

    yh = parts.shape[0]
    strips = yh // 2
    for b in range(strips):
        both = parts[2 * b + 1] + parts[(2 * b + 2) % yh]
        for z in range(2):
            inner = both[z, 4:12].sum(axis=0, keepdims=True)
            outer = both[z].sum(axis=0, keepdims=True) - inner
            sums[z, 2 * b : 2 * b + 1] = inner
            sums[z, 2 * b + 1 : 2 * b + 2] = outer
    pl.semaphore_wait(barrier, n - 1)
    copy = pltpu.make_async_remote_copy(
        src_ref=sums.at[0],
        dst_ref=arrived,
        send_sem=halo_send,
        recv_sem=halo_recv,
        device_id={"slab": lax.rem(me + n - 1, n)},
        device_id_type=pl.DeviceIdType.MESH,
    )
    copy.start()
    copy.wait()
    gain = g1[...]
    carrier = (sums[1] + arrived[...]) * (1.0 / WIN**3)
    count = carrier.shape[0]
    normed = norm(carrier, gain).astype(jnp.bfloat16)
    proj = jnp.dot(normed, wc[...], preferred_element_type=jnp.float32)
    proj = proj.astype(jnp.bfloat16).astype(jnp.float32)
    everyone[me] = proj[:, C:]

    def peer(d):
        return pltpu.make_async_remote_copy(
            src_ref=everyone.at[me],
            dst_ref=everyone.at[me],
            send_sem=send_sem.at[d],
            recv_sem=recv_sem.at[d],
            device_id={"slab": lax.rem(me + d, n)},
            device_id_type=pl.DeviceIdType.MESH,
        )

    @pl.loop(1, n)
    def _(d):
        peer(d).start()

    @pl.loop(1, n)
    def _(d):
        peer(d).wait()

    kv = everyone[...].reshape(n * count, 2 * C).astype(jnp.bfloat16)
    lane = lax.broadcasted_iota(jnp.int32, (count, C), 1) // HD
    asking = jnp.concatenate(
        [jnp.where(lane == h, proj[:, :C], 0.0) for h in range(HEADS)], axis=0
    ).astype(jnp.bfloat16)
    s = dot_t(asking, kv[:, :C]) * HD**-0.5
    p = jnp.exp(s - jnp.max(s, axis=1, keepdims=True))
    p = p / jnp.sum(p, axis=1, keepdims=True)
    high = p.astype(jnp.bfloat16)
    low = (p - high.astype(jnp.float32)).astype(jnp.bfloat16)
    wide = jnp.dot(high, kv[:, C:], preferred_element_type=jnp.float32) + jnp.dot(
        low, kv[:, C:], preferred_element_type=jnp.float32
    )
    mix = jnp.zeros((count, C), jnp.float32)
    for h in range(HEADS):
        mix = jnp.where(lane == h, wide[h * count : (h + 1) * count], mix)
    delta = jnp.dot(mix.astype(jnp.bfloat16), wco[...], preferred_element_type=jnp.float32)
    delta_out[...] = delta
    own = jnp.dot(
        norm(carrier + delta, gain).astype(jnp.bfloat16),
        wr[:, C:],
        preferred_element_type=jnp.float32,
    )
    own = own.astype(jnp.bfloat16).astype(jnp.float32)
    kc_out[...] = own[:, :C]
    vc_out[...] = own[:, C:]


def carriers(parts, g1, wc, wco, wr):
    n = lax.axis_size("slab")
    count = parts.shape[0]
    shape = jax.ShapeDtypeStruct((count, C), jnp.float32)
    return pl.pallas_call(
        functools.partial(carrier_kernel, n),
        out_shape=(shape,) * 3,
        in_specs=[pl.BlockSpec(memory_space=pltpu.VMEM)] * 5,
        out_specs=(pl.BlockSpec(memory_space=pltpu.VMEM),) * 3,
        scratch_shapes=[
            pltpu.VMEM((2, count, C), jnp.float32),
            pltpu.VMEM((count, C), jnp.float32),
            pltpu.VMEM((n, count, 2 * C), jnp.float32),
            pltpu.SemaphoreType.DMA,
            pltpu.SemaphoreType.DMA,
            pltpu.SemaphoreType.DMA((n,)),
            pltpu.SemaphoreType.DMA((n,)),
        ],
        compiler_params=pltpu.CompilerParams(
            collective_id=0, has_side_effects=True, vmem_limit_bytes=24 * 1024 * 1024
        ),
        cost_estimate=pl.CostEstimate(
            flops=10**9, bytes_accessed=30 * 10**6, transcendentals=20000
        ),
        name="carriers",
    )(parts, g1, wc, wco, wr)


def body(volume_features, g1, g2, wc, wco, wr, wro, w1, w2):
    planes, ny, nx, channels = volume_features.shape
    yh = ny // HALF
    strips = yh // 2
    volume = volume_features.reshape(planes, yh, HALF * nx, channels)
    position = lax.axis_index("slab")
    last = (position == lax.axis_size("slab") - 1).astype(jnp.int32).reshape(1)
    cuts = [(0, strips - 1), (strips - 1, strips)]
    halos = []
    for lo, hi in cuts:
        if hi < strips:
            sent = volume[:HALF, 2 * lo + 1 : 2 * hi + 1]
        else:
            sent = jnp.concatenate([volume[:HALF, 2 * lo + 1 :], volume[:HALF, :1]], axis=1)
        halos.append(shifted(sent, "slab", -1))
    gains = (g1.reshape(1, channels), g2.reshape(1, channels))
    delta, kc, vc = carriers(half_sums(volume), gains[0], wc, wco, wr)
    ws = (wr, wro, w1, w2)
    local, returned = [], []
    for (lo, hi), halo in zip(cuts, halos):
        out_loc, out_halo = strips_call(
            lo, hi - lo, strips, last, volume, halo, 0, *gains, ws, delta, kc, vc
        )
        local.append(out_loc)
        returned.append(shifted(out_halo, "slab", 1))
    local = jnp.concatenate([local[-1][:, -1:]] + local[:-1] + [local[-1][:, :-1]], axis=1)
    returned = jnp.concatenate(
        [returned[-1][:, -1:]] + returned[:-1] + [returned[-1][:, :-1]], axis=1
    )
    done = jnp.concatenate([returned, local], axis=0)
    return done.reshape(volume_features.shape)


def solution(mesh):
    placed = (P(("groups", "slab"), None, None, None),) + (P(),) * 8
    return jax.shard_map(
        body,
        mesh=mesh,
        in_specs=placed,
        out_specs=P(("groups", "slab"), None, None, None),
        check_vma=False,
    )
```

```python
import functools

import jax
import jax.numpy as jnp
from jax import lax
from jax.experimental import pallas as pl
from jax.experimental.pallas import tpu as pltpu
from jax.sharding import PartitionSpec as P

C = 384
HEADS = 12
HD = 32
WIN = 8
HALF = 4
GROUPS = C // 128
BIG = 2.0**100
LOG2E = 1.4426950408889634


def shifted(value, axis, steps):
    count = lax.axis_size(axis)
    pairs = [(source, (source + steps) % count) for source in range(count)]
    return lax.ppermute(value, axis, pairs)


def norm(values, gain):
    values = values.astype(jnp.float32)
    centre = jnp.mean(values, axis=-1, keepdims=True)
    moved = values - centre
    spread = jnp.mean(moved * moved, axis=-1, keepdims=True)
    return moved * lax.rsqrt(spread + 1e-05) * gain


def dot_t(a, b):
    return lax.dot_general(a, b, (((1,), (1,)), ((), ())), preferred_element_type=jnp.float32)


def row_of(values, row):
    at = lax.broadcasted_iota(jnp.int32, values.shape, 0)
    return jnp.sum(jnp.where(at == row, values, 0.0), axis=0, keepdims=True)


def strip_kernel(
    first,
    strips,
    last_ref,
    loc_a,
    loc_b,
    halo_a,
    halo_b,
    g1,
    g2,
    wqkv,
    wo,
    w1,
    w2,
    wvt,
    delta,
    kc,
    vc,
    out_loc,
    out_halo,
    x_s,
    qkv_s,
    vt_s,
    att_s,
    y_s,
):
    strip = pl.program_id(0) + first
    rows = 2 * WIN**3
    half = WIN**3
    tokens = jnp.concatenate(
        [r[...].reshape(rows // 4, C).astype(jnp.float32) for r in (loc_a, loc_b, halo_a, halo_b)],
        axis=0,
    )
    tokens = pltpu.roll(tokens, rows - HALF, 0).reshape(rows // 16, 2, 8, C)
    gain1 = g1[...]
    for w in range(2):
        x_w = tokens[:, w].reshape(half, C)
        x_s[w] = x_w
        n_w = norm(x_w, gain1).astype(jnp.bfloat16)
        vt = dot_t(wvt[...], n_w).astype(jnp.bfloat16)
        for g in range(GROUPS):
            vt_s[w, g] = vt[g * 128 : (g + 1) * 128]
        for part in range(2):
            proj = jnp.dot(
                n_w, wqkv[:, part * C : (part + 1) * C], preferred_element_type=jnp.float32
            )
            if part == 0:
                proj = proj * (HD**-0.5 * LOG2E)
            proj = proj.astype(jnp.bfloat16)
            for g in range(GROUPS):
                qkv_s[part, w, g] = proj[:, g * 128 : (g + 1) * 128]

    lane = lax.broadcasted_iota(jnp.int32, (1, 128), 1)
    zflag = last_ref[0]
    yflag = jnp.where(strip == strips - 1, 1, 0)

    def attend(step, carry):
        w = step // GROUPS
        g = step % GROUPS
        row = lax.broadcasted_iota(jnp.int32, (half, 128), 0)
        col = lax.broadcasted_iota(jnp.int32, (half, 128), 1)
        t = ((row // 8) * 16 + row % 8 + w * 8 + HALF) & (rows - 1)
        label = (
            (t // half) * 4 * zflag
            + ((t // (half // 2)) & 1) * 2 * yflag
            + jnp.where((t & 15) < HALF, w, 0)
        )
        same = label == col
        feat_q = jnp.where(same, 0.0, -BIG).astype(jnp.bfloat16)
        feat_k = jnp.where(same, 1.0, 0.0).astype(jnp.bfloat16)
        q4 = qkv_s[0, w, g]
        vt4 = vt_s[w, g]
        k_aug = jnp.concatenate([qkv_s[1, w, g], feat_k], axis=1)
        lanes = pl.ds(pl.multiple_of(g * 128, 128), 128)
        kcw = row_of(kc[:, lanes], 2 * strip + w)
        vcw = row_of(vc[:, lanes], 2 * strip + w)
        r16 = lax.broadcasted_iota(jnp.int32, (16, 128), 0)
        k_rows = jnp.where(lane // HD == r16, kcw, 0.0).astype(jnp.bfloat16)
        affinity = dot_t(k_rows, q4)
        r128 = lax.broadcasted_iota(jnp.int32, (128, 128), 0)
        v_col = jnp.sum(jnp.where(r128 == lane, vcw, 0.0), axis=1, keepdims=True)
        ones = jnp.ones((16, half), jnp.bfloat16)
        blocks = []
        for h in range(4):
            mask = jnp.where((lane // HD) == h, 1.0, 0.0).astype(jnp.bfloat16)
            q_aug = jnp.concatenate([q4 * mask, feat_q], axis=1)
            s = dot_t(k_aug, q_aug)
            m = jnp.max(s, axis=0, keepdims=True)
            p = jnp.exp2(s - m).astype(jnp.bfloat16)
            own = slice(h * HD, (h + 1) * HD)
            vt = jnp.concatenate([vt4[own], ones], axis=0)
            o = jnp.dot(vt, p, preferred_element_type=jnp.float32)
            c = affinity[h : h + 1]
            top = jnp.maximum(m, c)
            a = jnp.exp2(m - top)
            e = jnp.exp2(c - top)
            blocks.append((o[:HD] * a + e * v_col[own]) / (o[HD : HD + 1] * a + e))
        att_s[w, g] = jnp.concatenate(blocks, axis=0).T.astype(jnp.bfloat16)
        return carry

    lax.fori_loop(0, 2 * GROUPS, attend, 0, unroll=3)

    gain2 = g2[...]
    tile = half // 2

    def finish(step, carry):
        w = step // 2
        part = step % 2
        at = pl.ds(pl.multiple_of(part * tile, tile), tile)
        att = jnp.concatenate([att_s[w, g, at] for g in range(GROUPS)], axis=1)
        mixed = x_s[w, at] + jnp.dot(att, wo[...], preferred_element_type=jnp.float32)
        mixed = (mixed + row_of(delta[...], 2 * strip + w)).astype(jnp.bfloat16).astype(jnp.float32)
        n = norm(mixed, gain2).astype(jnp.bfloat16)
        u = jnp.dot(n, w1[...], preferred_element_type=jnp.float32)
        hidden = 0.5 * u * (1.0 + jnp.tanh((2.0 / jnp.pi) ** 0.5 * (u + 0.044715 * (u * u * u))))
        out = mixed + jnp.dot(
            hidden.astype(jnp.bfloat16), w2[...], preferred_element_type=jnp.float32
        )
        y_s[pl.ds(part * (tile // 8), tile // 8), w] = out.reshape(tile // 8, 8, C)
        return carry

    lax.fori_loop(0, 4, finish, 0)
    done = pltpu.roll(y_s[...].reshape(rows, C), HALF, 0).astype(jnp.bfloat16)
    done = done.reshape(4, HALF, HALF * 16, C)
    ya = 2 * pl.program_id(0)
    out_loc[:, ya] = done[0]
    out_loc[:, ya + 1] = done[1]
    out_halo[:, ya] = done[2]
    out_halo[:, ya + 1] = done[3]


def strips_call(first, count, strips, last, volume, halo, halo_first, g1, g2, ws, delta, kc, vc):
    yh = 2 * strips

    def block(plane, offset):
        return pl.BlockSpec(
            (HALF, 1, HALF * 16, C), lambda b: (plane, (2 * (b + first) + offset) % yh, 0, 0)
        )

    def halo_block(offset):
        return pl.BlockSpec((HALF, 1, HALF * 16, C), lambda b: (0, 2 * b + offset + halo_first, 0, 0))

    def whole(a):
        return pl.BlockSpec(a.shape, lambda b: (0,) * a.ndim)

    half = WIN**3
    shape = jax.ShapeDtypeStruct((HALF, 2 * count, HALF * 16, C), jnp.bfloat16)
    out_spec = pl.BlockSpec(shape.shape, lambda b: (0, 0, 0, 0))
    flops = count * 2 * half * 2 * (C * 3 * C + C * C + 2 * C * 4 * C + HEADS * half * 320)
    return pl.pallas_call(
        functools.partial(strip_kernel, first, strips),
        grid=(count,),
        out_shape=(shape, shape),
        in_specs=[
            pl.BlockSpec(memory_space=pltpu.SMEM),
            block(1, 1),
            block(1, 2),
            halo_block(0),
            halo_block(1),
            whole(g1),
            whole(g2),
        ]
        + [whole(w) for w in (*ws, delta, kc, vc)],
        out_specs=(out_spec, out_spec),
        scratch_shapes=[
            pltpu.VMEM((2, half, C), jnp.float32),
            pltpu.VMEM((2, 2, GROUPS, half, 128), jnp.bfloat16),
            pltpu.VMEM((2, GROUPS, 128, half), jnp.bfloat16),
            pltpu.VMEM((2, GROUPS, half, 128), jnp.bfloat16),
            pltpu.VMEM((2 * half // 16, 2, 8, C), jnp.float32),
        ],
        compiler_params=pltpu.CompilerParams(
            dimension_semantics=("arbitrary",), vmem_limit_bytes=48 * 1024 * 1024
        ),
        cost_estimate=pl.CostEstimate(
            flops=flops,
            bytes_accessed=count * 4 * 2 * half * C * 2,
            transcendentals=count * 2 * half * (HEADS * half + 4 * C),
        ),
        name="strips",
    )(last, volume, volume, halo, halo, g1, g2, *ws, delta, kc, vc)


def sums_kernel(volume, out):
    planes = volume.shape[0]
    block = volume[:, 0].astype(jnp.float32)
    out[0] = block.reshape(planes // HALF, HALF * HALF, 16, C).sum(axis=1)


def half_sums(volume):
    planes, yh = volume.shape[:2]
    return pl.pallas_call(
        sums_kernel,
        grid=(yh,),
        out_shape=jax.ShapeDtypeStruct((yh, planes // HALF, 16, C), jnp.float32),
        in_specs=[pl.BlockSpec((planes, 1, HALF * 16, C), lambda y: (0, y, 0, 0))],
        out_specs=pl.BlockSpec((1, planes // HALF, 16, C), lambda y: (y, 0, 0, 0)),
        cost_estimate=pl.CostEstimate(
            flops=2 * volume.size, bytes_accessed=2 * volume.size, transcendentals=0
        ),
        name="half_sums",
    )(volume)


def carrier_kernel(
    n, parts, g1, wc, wco, wr, delta_out, kc_out, vc_out,
    sums, arrived, everyone, halo_send, halo_recv, send_sem, recv_sem,
):
    me = lax.axis_index("slab")
    barrier = pltpu.get_barrier_semaphore()

    @pl.loop(1, n)
    def _(d):
        pl.semaphore_signal(
            barrier, inc=1, device_id={"slab": lax.rem(me + d, n)}, device_id_type=pl.DeviceIdType.MESH
        )

    yh = parts.shape[0]
    strips = yh // 2
    for b in range(strips):
        both = parts[2 * b + 1] + parts[(2 * b + 2) % yh]
        for z in range(2):
            inner = both[z, 4:12].sum(axis=0, keepdims=True)
            outer = both[z].sum(axis=0, keepdims=True) - inner
            sums[z, 2 * b : 2 * b + 1] = inner
            sums[z, 2 * b + 1 : 2 * b + 2] = outer
    pl.semaphore_wait(barrier, n - 1)
    copy = pltpu.make_async_remote_copy(
        src_ref=sums.at[0],
        dst_ref=arrived,
        send_sem=halo_send,
        recv_sem=halo_recv,
        device_id={"slab": lax.rem(me + n - 1, n)},
        device_id_type=pl.DeviceIdType.MESH,
    )
    copy.start()
    copy.wait()
    gain = g1[...]
    carrier = (sums[1] + arrived[...]) * (1.0 / WIN**3)
    count = carrier.shape[0]
    normed = norm(carrier, gain).astype(jnp.bfloat16)
    proj = jnp.dot(normed, wc[...], preferred_element_type=jnp.float32)
    proj = proj.astype(jnp.bfloat16).astype(jnp.float32)
    everyone[me] = proj[:, C:]

    def peer(d):
        return pltpu.make_async_remote_copy(
            src_ref=everyone.at[me],
            dst_ref=everyone.at[me],
            send_sem=send_sem.at[d],
            recv_sem=recv_sem.at[d],
            device_id={"slab": lax.rem(me + d, n)},
            device_id_type=pl.DeviceIdType.MESH,
        )

    @pl.loop(1, n)
    def _(d):
        peer(d).start()

    @pl.loop(1, n)
    def _(d):
        peer(d).wait()

    kv = everyone[...].reshape(n * count, 2 * C).astype(jnp.bfloat16)
    lane = lax.broadcasted_iota(jnp.int32, (count, C), 1) // HD
    asking = jnp.concatenate(
        [jnp.where(lane == h, proj[:, :C], 0.0) for h in range(HEADS)], axis=0
    ).astype(jnp.bfloat16)
    s = dot_t(asking, kv[:, :C]) * HD**-0.5
    p = jnp.exp(s - jnp.max(s, axis=1, keepdims=True))
    p = p / jnp.sum(p, axis=1, keepdims=True)
    high = p.astype(jnp.bfloat16)
    low = (p - high.astype(jnp.float32)).astype(jnp.bfloat16)
    wide = jnp.dot(high, kv[:, C:], preferred_element_type=jnp.float32) + jnp.dot(
        low, kv[:, C:], preferred_element_type=jnp.float32
    )
    mix = jnp.zeros((count, C), jnp.float32)
    for h in range(HEADS):
        mix = jnp.where(lane == h, wide[h * count : (h + 1) * count], mix)
    delta = jnp.dot(mix.astype(jnp.bfloat16), wco[...], preferred_element_type=jnp.float32)
    delta_out[...] = delta
    own = jnp.dot(
        norm(carrier + delta, gain).astype(jnp.bfloat16),
        wr[:, C:],
        preferred_element_type=jnp.float32,
    )
    own = own.astype(jnp.bfloat16).astype(jnp.float32)
    kc_out[...] = own[:, :C]
    vc_out[...] = own[:, C:]


def carriers(parts, g1, wc, wco, wr):
    n = lax.axis_size("slab")
    count = parts.shape[0]
    shape = jax.ShapeDtypeStruct((count, C), jnp.float32)
    return pl.pallas_call(
        functools.partial(carrier_kernel, n),
        out_shape=(shape,) * 3,
        in_specs=[pl.BlockSpec(memory_space=pltpu.VMEM)] * 5,
        out_specs=(pl.BlockSpec(memory_space=pltpu.VMEM),) * 3,
        scratch_shapes=[
            pltpu.VMEM((2, count, C), jnp.float32),
            pltpu.VMEM((count, C), jnp.float32),
            pltpu.VMEM((n, count, 2 * C), jnp.float32),
            pltpu.SemaphoreType.DMA,
            pltpu.SemaphoreType.DMA,
            pltpu.SemaphoreType.DMA((n,)),
            pltpu.SemaphoreType.DMA((n,)),
        ],
        compiler_params=pltpu.CompilerParams(
            collective_id=0, has_side_effects=True, vmem_limit_bytes=24 * 1024 * 1024
        ),
        cost_estimate=pl.CostEstimate(
            flops=10**9, bytes_accessed=30 * 10**6, transcendentals=20000
        ),
        name="carriers",
    )(parts, g1, wc, wco, wr)


def body(volume_features, g1, g2, wc, wco, wr, wro, w1, w2):
    planes, ny, nx, channels = volume_features.shape
    yh = ny // HALF
    strips = yh // 2
    volume = volume_features.reshape(planes, yh, HALF * nx, channels)
    position = lax.axis_index("slab")
    last = (position == lax.axis_size("slab") - 1).astype(jnp.int32).reshape(1)
    cuts = [(0, strips - 1), (strips - 1, strips)]
    halos = []
    for lo, hi in cuts:
        if hi < strips:
            sent = volume[:HALF, 2 * lo + 1 : 2 * hi + 1]
        else:
            sent = jnp.concatenate([volume[:HALF, 2 * lo + 1 :], volume[:HALF, :1]], axis=1)
        halos.append(shifted(sent, "slab", -1))
    gains = (g1.reshape(1, channels), g2.reshape(1, channels))
    delta, kc, vc = carriers(half_sums(volume), gains[0], wc, wco, wr)
    ws = (wr, wro, w1, w2, wr[:, 2 * channels :].T)
    local, returned = [], []
    for (lo, hi), halo in zip(cuts, halos):
        out_loc, out_halo = strips_call(
            lo, hi - lo, strips, last, volume, halo, 0, *gains, ws, delta, kc, vc
        )
        local.append(out_loc)
        returned.append(shifted(out_halo, "slab", 1))
    local = jnp.concatenate([local[-1][:, -1:]] + local[:-1] + [local[-1][:, :-1]], axis=1)
    returned = jnp.concatenate(
        [returned[-1][:, -1:]] + returned[:-1] + [returned[-1][:, :-1]], axis=1
    )
    done = jnp.concatenate([returned, local], axis=0)
    return done.reshape(volume_features.shape)


def solution(mesh):
    placed = (P(("groups", "slab"), None, None, None),) + (P(),) * 8
    return jax.shard_map(
        body,
        mesh=mesh,
        in_specs=placed,
        out_specs=P(("groups", "slab"), None, None, None),
        check_vma=False,
    )
```

```python
import functools

import jax
import jax.numpy as jnp
from jax import lax
from jax.experimental import pallas as pl
from jax.experimental.pallas import tpu as pltpu
from jax.sharding import PartitionSpec as P

C = 384
HEADS = 12
HD = 32
WIN = 8
HALF = 4
GROUPS = C // 128
BIG = 2.0**100
LOG2E = 1.4426950408889634


def shifted(value, axis, steps):
    count = lax.axis_size(axis)
    pairs = [(source, (source + steps) % count) for source in range(count)]
    return lax.ppermute(value, axis, pairs)


def norm(values, gain):
    values = values.astype(jnp.float32)
    centre = jnp.mean(values, axis=-1, keepdims=True)
    moved = values - centre
    spread = jnp.mean(moved * moved, axis=-1, keepdims=True)
    return moved * lax.rsqrt(spread + 1e-05) * gain


def dot_t(a, b):
    return lax.dot_general(a, b, (((1,), (1,)), ((), ())), preferred_element_type=jnp.float32)


def row_of(values, row):
    at = lax.broadcasted_iota(jnp.int32, values.shape, 0)
    return jnp.sum(jnp.where(at == row, values, 0.0), axis=0, keepdims=True)


def strip_kernel(
    first,
    strips,
    last_ref,
    loc_a,
    loc_b,
    halo_a,
    halo_b,
    g1,
    g2,
    wqkv,
    wo,
    w1,
    w2,
    delta,
    kc,
    vc,
    out_loc,
    out_halo,
    x_s,
    qkv_s,
    att_s,
    y_s,
):
    strip = pl.program_id(0) + first
    rows = 2 * WIN**3
    half = WIN**3
    tokens = jnp.concatenate(
        [r[...].reshape(rows // 4, C).astype(jnp.float32) for r in (loc_a, loc_b, halo_a, halo_b)],
        axis=0,
    )
    tokens = pltpu.roll(tokens, rows - HALF, 0).reshape(rows // 16, 2, 8, C)
    gain1 = g1[...]
    for w in range(2):
        x_w = tokens[:, w].reshape(half, C)
        x_s[w] = x_w
        n_w = norm(x_w, gain1).astype(jnp.bfloat16)
        for part in range(3):
            proj = jnp.dot(
                n_w, wqkv[:, part * C : (part + 1) * C], preferred_element_type=jnp.float32
            )
            if part == 0:
                proj = proj * (HD**-0.5 * LOG2E)
            proj = proj.astype(jnp.bfloat16)
            for g in range(GROUPS):
                qkv_s[part, w, g] = proj[:, g * 128 : (g + 1) * 128]

    lane = lax.broadcasted_iota(jnp.int32, (1, 128), 1)
    zflag = last_ref[0]
    yflag = jnp.where(strip == strips - 1, 1, 0)

    def attend(step, carry):
        w = step // GROUPS
        g = step % GROUPS
        row = lax.broadcasted_iota(jnp.int32, (half, 128), 0)
        col = lax.broadcasted_iota(jnp.int32, (half, 128), 1)
        t = ((row // 8) * 16 + row % 8 + w * 8 + HALF) & (rows - 1)
        label = (
            (t // half) * 4 * zflag
            + ((t // (half // 2)) & 1) * 2 * yflag
            + jnp.where((t & 15) < HALF, w, 0)
        )
        same = label == col
        feat_q = jnp.where(same, 0.0, -BIG).astype(jnp.bfloat16)
        feat_k = jnp.where(same, 1.0, 0.0).astype(jnp.bfloat16)
        q4 = qkv_s[0, w, g]
        k4 = qkv_s[1, w, g]
        v4 = qkv_s[2, w, g]
        k_aug = jnp.concatenate([k4, feat_k], axis=1)
        weights, contents = [], []
        peak = jnp.zeros((half, 128), jnp.float32)
        zero = jnp.zeros((), jnp.bfloat16)
        for h in range(4):
            mine = (lane // HD) == h
            mask = jnp.where(mine, 1.0, 0.0).astype(jnp.bfloat16)
            q_aug = jnp.concatenate([q4 * mask, feat_q], axis=1)
            s = dot_t(q_aug, k_aug)
            m = jnp.max(s, axis=1, keepdims=True)
            p = jnp.exp2(s - m).astype(jnp.bfloat16)
            v_aug = jnp.concatenate([v4 * mask, jnp.broadcast_to(mask, (half, 128))], axis=1)
            weights.append(p)
            contents.append(v_aug)
            peak = jnp.where(mine, m, peak)
        acc = jnp.dot(
            jnp.concatenate(weights, axis=1),
            jnp.concatenate(contents, axis=0),
            preferred_element_type=jnp.float32,
        )
        lanes = pl.ds(pl.multiple_of(g * 128, 128), 128)
        kcw = row_of(kc[:, lanes], 2 * strip + w)
        vcw = row_of(vc[:, lanes], 2 * strip + w)
        r128 = lax.broadcasted_iota(jnp.int32, (128, 128), 0)
        c128 = lax.broadcasted_iota(jnp.int32, (128, 128), 1)
        k_mat = jnp.where(r128 // HD == c128 // HD, kcw, 0.0).astype(jnp.bfloat16)
        c4 = dot_t(q4, k_mat)
        top = jnp.maximum(peak, c4)
        a = jnp.exp2(peak - top)
        e = jnp.exp2(c4 - top)
        att = (acc[:, :128] * a + e * vcw) / (acc[:, 128:] * a + e)
        att_s[w, g] = att.astype(jnp.bfloat16)
        return carry

    lax.fori_loop(0, 2 * GROUPS, attend, 0, unroll=True)

    gain2 = g2[...]
    tile = half // 2

    def finish(step, carry):
        w = step // 2
        part = step % 2
        at = pl.ds(pl.multiple_of(part * tile, tile), tile)
        att = jnp.concatenate([att_s[w, g, at] for g in range(GROUPS)], axis=1)
        mixed = x_s[w, at] + jnp.dot(att, wo[...], preferred_element_type=jnp.float32)
        mixed = (mixed + row_of(delta[...], 2 * strip + w)).astype(jnp.bfloat16).astype(jnp.float32)
        n = norm(mixed, gain2).astype(jnp.bfloat16)
        u = jnp.dot(n, w1[...], preferred_element_type=jnp.float32)
        hidden = 0.5 * u * (1.0 + jnp.tanh((2.0 / jnp.pi) ** 0.5 * (u + 0.044715 * (u * u * u))))
        out = mixed + jnp.dot(
            hidden.astype(jnp.bfloat16), w2[...], preferred_element_type=jnp.float32
        )
        y_s[pl.ds(part * (tile // 8), tile // 8), w] = out.reshape(tile // 8, 8, C)
        return carry

    lax.fori_loop(0, 4, finish, 0, unroll=True)
    done = pltpu.roll(y_s[...].reshape(rows, C), HALF, 0).astype(jnp.bfloat16)
    done = done.reshape(4, HALF, HALF * 16, C)
    ya = 2 * pl.program_id(0)
    out_loc[:, ya] = done[0]
    out_loc[:, ya + 1] = done[1]
    out_halo[:, ya] = done[2]
    out_halo[:, ya + 1] = done[3]


def strips_call(first, count, strips, last, volume, halo, halo_first, g1, g2, ws, delta, kc, vc):
    yh = 2 * strips

    def block(plane, offset):
        return pl.BlockSpec(
            (HALF, 1, HALF * 16, C), lambda b: (plane, (2 * (b + first) + offset) % yh, 0, 0)
        )

    def halo_block(offset):
        return pl.BlockSpec((HALF, 1, HALF * 16, C), lambda b: (0, 2 * b + offset + halo_first, 0, 0))

    def whole(a):
        return pl.BlockSpec(a.shape, lambda b: (0,) * a.ndim)

    half = WIN**3
    shape = jax.ShapeDtypeStruct((HALF, 2 * count, HALF * 16, C), jnp.bfloat16)
    out_spec = pl.BlockSpec(shape.shape, lambda b: (0, 0, 0, 0))
    flops = count * 2 * half * 2 * (C * 3 * C + C * C + 2 * C * 4 * C + HEADS * half * 320)
    return pl.pallas_call(
        functools.partial(strip_kernel, first, strips),
        grid=(count,),
        out_shape=(shape, shape),
        in_specs=[
            pl.BlockSpec(memory_space=pltpu.SMEM),
            block(1, 1),
            block(1, 2),
            halo_block(0),
            halo_block(1),
            whole(g1),
            whole(g2),
        ]
        + [whole(w) for w in (*ws, delta, kc, vc)],
        out_specs=(out_spec, out_spec),
        scratch_shapes=[
            pltpu.VMEM((2, half, C), jnp.float32),
            pltpu.VMEM((3, 2, GROUPS, half, 128), jnp.bfloat16),
            pltpu.VMEM((2, GROUPS, half, 128), jnp.bfloat16),
            pltpu.VMEM((2 * half // 16, 2, 8, C), jnp.float32),
        ],
        compiler_params=pltpu.CompilerParams(
            dimension_semantics=("arbitrary",), vmem_limit_bytes=48 * 1024 * 1024
        ),
        cost_estimate=pl.CostEstimate(
            flops=flops,
            bytes_accessed=count * 4 * 2 * half * C * 2,
            transcendentals=count * 2 * half * (HEADS * half + 4 * C),
        ),
        name="strips",
    )(last, volume, volume, halo, halo, g1, g2, *ws, delta, kc, vc)


def sums_kernel(volume, out):
    planes = volume.shape[0]
    block = volume[:, 0].astype(jnp.float32)
    out[0] = block.reshape(planes // HALF, HALF * HALF, 16, C).sum(axis=1)


def half_sums(volume):
    planes, yh = volume.shape[:2]
    return pl.pallas_call(
        sums_kernel,
        grid=(yh,),
        out_shape=jax.ShapeDtypeStruct((yh, planes // HALF, 16, C), jnp.float32),
        in_specs=[pl.BlockSpec((planes, 1, HALF * 16, C), lambda y: (0, y, 0, 0))],
        out_specs=pl.BlockSpec((1, planes // HALF, 16, C), lambda y: (y, 0, 0, 0)),
        cost_estimate=pl.CostEstimate(
            flops=2 * volume.size, bytes_accessed=2 * volume.size, transcendentals=0
        ),
        name="half_sums",
    )(volume)


def carrier_kernel(
    n, parts, g1, wc, wco, wr, delta_out, kc_out, vc_out,
    sums, arrived, everyone, halo_send, halo_recv, send_sem, recv_sem,
):
    me = lax.axis_index("slab")
    barrier = pltpu.get_barrier_semaphore()

    @pl.loop(1, n)
    def _(d):
        pl.semaphore_signal(
            barrier, inc=1, device_id={"slab": lax.rem(me + d, n)}, device_id_type=pl.DeviceIdType.MESH
        )

    yh = parts.shape[0]
    strips = yh // 2
    for b in range(strips):
        both = parts[2 * b + 1] + parts[(2 * b + 2) % yh]
        for z in range(2):
            inner = both[z, 4:12].sum(axis=0, keepdims=True)
            outer = both[z].sum(axis=0, keepdims=True) - inner
            sums[z, 2 * b : 2 * b + 1] = inner
            sums[z, 2 * b + 1 : 2 * b + 2] = outer
    pl.semaphore_wait(barrier, n - 1)
    copy = pltpu.make_async_remote_copy(
        src_ref=sums.at[0],
        dst_ref=arrived,
        send_sem=halo_send,
        recv_sem=halo_recv,
        device_id={"slab": lax.rem(me + n - 1, n)},
        device_id_type=pl.DeviceIdType.MESH,
    )
    copy.start()
    copy.wait()
    gain = g1[...]
    carrier = (sums[1] + arrived[...]) * (1.0 / WIN**3)
    count = carrier.shape[0]
    normed = norm(carrier, gain).astype(jnp.bfloat16)
    proj = jnp.dot(normed, wc[...], preferred_element_type=jnp.float32)
    proj = proj.astype(jnp.bfloat16).astype(jnp.float32)
    everyone[me] = proj[:, C:]

    def peer(d):
        return pltpu.make_async_remote_copy(
            src_ref=everyone.at[me],
            dst_ref=everyone.at[me],
            send_sem=send_sem.at[d],
            recv_sem=recv_sem.at[d],
            device_id={"slab": lax.rem(me + d, n)},
            device_id_type=pl.DeviceIdType.MESH,
        )

    @pl.loop(1, n)
    def _(d):
        peer(d).start()

    @pl.loop(1, n)
    def _(d):
        peer(d).wait()

    kv = everyone[...].reshape(n * count, 2 * C).astype(jnp.bfloat16)
    lane = lax.broadcasted_iota(jnp.int32, (count, C), 1) // HD
    asking = jnp.concatenate(
        [jnp.where(lane == h, proj[:, :C], 0.0) for h in range(HEADS)], axis=0
    ).astype(jnp.bfloat16)
    s = dot_t(asking, kv[:, :C]) * HD**-0.5
    p = jnp.exp(s - jnp.max(s, axis=1, keepdims=True))
    p = p / jnp.sum(p, axis=1, keepdims=True)
    high = p.astype(jnp.bfloat16)
    low = (p - high.astype(jnp.float32)).astype(jnp.bfloat16)
    wide = jnp.dot(high, kv[:, C:], preferred_element_type=jnp.float32) + jnp.dot(
        low, kv[:, C:], preferred_element_type=jnp.float32
    )
    mix = jnp.zeros((count, C), jnp.float32)
    for h in range(HEADS):
        mix = jnp.where(lane == h, wide[h * count : (h + 1) * count], mix)
    delta = jnp.dot(mix.astype(jnp.bfloat16), wco[...], preferred_element_type=jnp.float32)
    delta_out[...] = delta
    own = jnp.dot(
        norm(carrier + delta, gain).astype(jnp.bfloat16),
        wr[:, C:],
        preferred_element_type=jnp.float32,
    )
    own = own.astype(jnp.bfloat16).astype(jnp.float32)
    kc_out[...] = own[:, :C]
    vc_out[...] = own[:, C:]


def carriers(parts, g1, wc, wco, wr):
    n = lax.axis_size("slab")
    count = parts.shape[0]
    shape = jax.ShapeDtypeStruct((count, C), jnp.float32)
    return pl.pallas_call(
        functools.partial(carrier_kernel, n),
        out_shape=(shape,) * 3,
        in_specs=[pl.BlockSpec(memory_space=pltpu.VMEM)] * 5,
        out_specs=(pl.BlockSpec(memory_space=pltpu.VMEM),) * 3,
        scratch_shapes=[
            pltpu.VMEM((2, count, C), jnp.float32),
            pltpu.VMEM((count, C), jnp.float32),
            pltpu.VMEM((n, count, 2 * C), jnp.float32),
            pltpu.SemaphoreType.DMA,
            pltpu.SemaphoreType.DMA,
            pltpu.SemaphoreType.DMA((n,)),
            pltpu.SemaphoreType.DMA((n,)),
        ],
        compiler_params=pltpu.CompilerParams(
            collective_id=0, has_side_effects=True, vmem_limit_bytes=24 * 1024 * 1024
        ),
        cost_estimate=pl.CostEstimate(
            flops=10**9, bytes_accessed=30 * 10**6, transcendentals=20000
        ),
        name="carriers",
    )(parts, g1, wc, wco, wr)


def body(volume_features, g1, g2, wc, wco, wr, wro, w1, w2):
    planes, ny, nx, channels = volume_features.shape
    yh = ny // HALF
    strips = yh // 2
    volume = volume_features.reshape(planes, yh, HALF * nx, channels)
    position = lax.axis_index("slab")
    last = (position == lax.axis_size("slab") - 1).astype(jnp.int32).reshape(1)
    cuts = [(0, strips - 1), (strips - 1, strips)]
    halos = []
    for lo, hi in cuts:
        if hi < strips:
            sent = volume[:HALF, 2 * lo + 1 : 2 * hi + 1]
        else:
            sent = jnp.concatenate([volume[:HALF, 2 * lo + 1 :], volume[:HALF, :1]], axis=1)
        halos.append(shifted(sent, "slab", -1))
    gains = (g1.reshape(1, channels), g2.reshape(1, channels))
    delta, kc, vc = carriers(half_sums(volume), gains[0], wc, wco, wr)
    ws = (wr, wro, w1, w2)
    local, returned = [], []
    for (lo, hi), halo in zip(cuts, halos):
        out_loc, out_halo = strips_call(
            lo, hi - lo, strips, last, volume, halo, 0, *gains, ws, delta, kc, vc
        )
        local.append(out_loc)
        returned.append(shifted(out_halo, "slab", 1))
    local = jnp.concatenate([local[-1][:, -1:]] + local[:-1] + [local[-1][:, :-1]], axis=1)
    returned = jnp.concatenate(
        [returned[-1][:, -1:]] + returned[:-1] + [returned[-1][:, :-1]], axis=1
    )
    done = jnp.concatenate([returned, local], axis=0)
    return done.reshape(volume_features.shape)


def solution(mesh):
    placed = (P(("groups", "slab"), None, None, None),) + (P(),) * 8
    return jax.shard_map(
        body,
        mesh=mesh,
        in_specs=placed,
        out_specs=P(("groups", "slab"), None, None, None),
        check_vma=False,
    )
```
